32 devices in a mesh: grp: 2 (over x), fin: 8 (over z, y), fout: 2 (over core).
Axes of the slice: x: 2, y: 2, z: 4, core: 2. Of those that a mesh axis runs over, the one named last changes fastest.
Arguments:
- tokens: bfloat16 [128, 6144], P(('grp', 'fin')), parts along dimension 0, may hold values from -6 to 6
- segment_ids: int32 [128], P(('grp', 'fin')), parts along dimension 0, may hold values from 0 to 3, never falling along the last dimension, each value on 1 to 32 neighbouring positions
- norm_gain: float32 [6144], replicated, may hold values from 0.1 to 1.9
- w_qkv: bfloat16 [6144, 3, 6144], P('fout', None, 'fin'), may hold values from -0.078125 to 0.078125
- w_up: bfloat16 [6144, 24576], P('fout', 'fin'), may hold values from -0.078125 to 0.078125
- w_out: bfloat16 [6144, 6144], P('fin', 'fout'), may hold values from -0.078125 to 0.078125
- w_down: bfloat16 [24576, 6144], P('fin', 'fout'), may hold values from -0.0390625 to 0.0390625
Outputs:
- layer_out: bfloat16 [128, 6144], P(('grp', 'fin'), 'fout'), parts along dimension 0
The draws below stay inside these ranges and needn't reach their ends.
There are 2 independent parts, one for each index of `grp`. The reference program is written for one: setup_inputs(seed, part) draws one part's arguments, and reference() takes and returns one part's arrays. A program takes and returns all parts, laid end to end along the dimension named above; an argument that names none is the same for every part. Nothing has to cross between parts.
Inputs may be any that keep to these rules, and one draw needn't show every extreme that they name: segment_ids never fall along the tokens; each image holds 1 to 32 consecutive tokens and some image holds exactly 32; every number from 0 to 3 names an image.
All inputs are finite; a program needn't handle non-finite values.
Results may differ from the reference program's by a relative error of at most 0.0052.
Values may be sent and summed in bfloat16 or wider, within the bound.
A program may use at most 192 MiB of HBM per device.

```python
import math
import jax
import jax.numpy as jnp
import numpy as np
from jax import lax

D = 6144
FF = 24576
HEADS = 48
HEAD = 128
TOKENS = 64
IMG_MOST = 32
IMAGES = 4


def levels(rng, shape, shards, low, top_value):
    def one(axis_at, shards_of):
        steps = jax.random.uniform(jax.random.fold_in(jax.random.fold_in(rng, 6), axis_at), (shards_of,), jnp.float32, low / len(shards), top_value / len(shards))
        return jnp.repeat(jnp.exp(steps), shape[axis_at] // shards_of).reshape((-1,) + (1,) * (len(shape) - axis_at - 1))

    loudness = one(*shards[0])
    for cut in shards[1:]:
        loudness = loudness * one(*cut)
    return loudness


def profile(number_of, total, limit, slope):
    loads = [(1 << 20) // math.isqrt(grade ** slope) + 1 for grade in range(2, number_of + 1)]
    surplus, holding = total - limit - (number_of - 1), [1] * (number_of - 1)
    while surplus > 0:
        movable = [i for i in range(number_of - 1) if holding[i] < limit]
        whole, left = sum([loads[i] for i in movable]), surplus
        for i in movable:
            addition = min(limit - holding[i], max(1, left * loads[i] // whole), surplus)
            holding[i] = holding[i] + addition
            surplus = surplus - addition
    return np.array([limit] + holding)


def ragged(own_key, number_of, total, bound, lean):
    if number_of == 2:
        one = jax.random.randint(own_key, (), max(1, total - bound), min(bound, total - 1) + 1)
        return jnp.stack([one, total - one])
    lengths = jnp.asarray(profile(number_of, total, bound, lean), jnp.int32)
    couples = (number_of - 1) // 2
    giver, sink = lengths[1:1 + 2 * couples:2], lengths[2:2 + 2 * couples:2]
    margin = jnp.minimum(giver - 1, bound - sink)
    passed = jax.random.randint(jax.random.fold_in(own_key, 1), (couples,), 0, 1 << 20) % (margin + 1)
    lengths = lengths.at[1:1 + 2 * couples:2].set(giver - passed).at[2:2 + 2 * couples:2].set(sink + passed)
    return lengths[jax.random.permutation(jax.random.fold_in(own_key, 2), number_of)]


def scatter_about(stream_key, shape, width, reach, split=(), dtype=jnp.bfloat16):
    result = width * jax.random.normal(stream_key, shape, jnp.float32)
    if split:
        result = result * levels(stream_key, shape, split, -0.22, 0.18)
    return jnp.clip(result, -reach, reach).astype(dtype)


def setup_inputs(seed: int = 0, part: int = 0) -> dict:
    streams_of = jax.random.split(jax.random.key(seed), 8)
    part_splits = jax.random.split(jax.random.fold_in(streams_of[7], part), 8)
    return {
        "tokens": scatter_about(part_splits[0], (TOKENS, D), 1.0, 6.0, ((0, 8),)),
        "segment_ids": jnp.searchsorted(jnp.cumsum(ragged(part_splits[1], IMAGES, TOKENS, IMG_MOST, 1)), jnp.arange(TOKENS), side="right").astype(jnp.int32),
        "norm_gain": jnp.clip(1.0 + 0.18 * jax.random.normal(streams_of[2], (D,), jnp.float32), 0.1, 1.9),
        "w_qkv": scatter_about(streams_of[3], (D, 3, D), D ** -0.5, 0.078125, ((0, 2), (2, 8))),
        "w_up": scatter_about(streams_of[4], (D, FF), D ** -0.5, 0.078125, ((0, 2), (1, 8))),
        "w_out": scatter_about(streams_of[5], (D, D), D ** -0.5, 0.078125, ((0, 8), (1, 2))),
        "w_down": scatter_about(streams_of[6], (FF, D), FF ** -0.5, 0.0390625, ((0, 8), (1, 2))),
    }


def feature_norm(values):
    center = lax.optimization_barrier(jnp.mean(values, -1, keepdims=True))
    square = lax.optimization_barrier(jnp.mean(values * values, -1, keepdims=True))
    return (values - center) * lax.rsqrt(square - center * center + 1e-06)

def reference(tokens, segment_ids, norm_gain, w_qkv, w_up, w_out, w_down):
    values = tokens.astype(jnp.float32)
    normed = (feature_norm(values) * norm_gain.astype(jnp.float32)).astype(jnp.bfloat16)
    qkv = jnp.dot(normed, w_qkv.reshape(D, 3 * D), preferred_element_type=jnp.float32).astype(jnp.bfloat16)
    qkv = qkv.reshape(TOKENS, 3, HEADS, HEAD)
    query = feature_norm(qkv[:, 0].astype(jnp.float32)).astype(jnp.bfloat16)
    keys = feature_norm(qkv[:, 1].astype(jnp.float32)).astype(jnp.bfloat16)
    value = qkv[:, 2]
    scores = jnp.einsum('qhd,khd->hqk', query.astype(jnp.float32), keys.astype(jnp.float32)) * (1.0 / math.sqrt(HEAD))
    same = segment_ids[:, None] == segment_ids[None, :]
    weight = jnp.where(same[None], jnp.exp(scores), 0.0).astype(jnp.bfloat16)
    den = lax.optimization_barrier(jnp.sum(weight.astype(jnp.float32), -1))
    total = jnp.einsum('hqk,khd->qhd', weight.astype(jnp.float32), value.astype(jnp.float32))
    attended = (total / jnp.transpose(den)[:, :, None]).astype(jnp.bfloat16)
    hidden = jax.nn.gelu(jnp.dot(normed, w_up, preferred_element_type=jnp.float32), approximate=False).astype(jnp.bfloat16)
    mixed = jnp.dot(attended.reshape(TOKENS, D), w_out, preferred_element_type=jnp.float32)
    mixed = mixed + jnp.dot(hidden, w_down, preferred_element_type=jnp.float32)
    return (values + mixed).astype(jnp.bfloat16)
```

```python
import functools
import math

import jax
import jax.numpy as jnp
from jax import lax
from jax.experimental import pallas as pl
from jax.experimental.pallas import tpu as pltpu
from jax.sharding import PartitionSpec as P

HEAD = 128
LANES = 128
TILE = 256
PAIR = 2
MESH = pl.DeviceIdType.MESH


def fused_kernel(
    lines, groups, chunks,
    tokens, ids, gain, wq, wu, wo, wd, out,
    wq_v, wu_v, wo_v, wd_v, xg, xs, idc, ps, pr, att, hid, p, ys, yr, zs, zr, own,
    wsem, gsend, grecv, psend, precv, ysend, yrecv, zsend, zrecv,
):
    rows, width = tokens.shape
    half = wu.shape[0]
    parts, _, cols = wq.shape
    count = lines * PAIR
    toks = rows * count
    up_w = wu.shape[1] // groups
    out_w = half // chunks
    me = lax.axis_index("fin")
    core = lax.axis_index("fout")
    z, y = lax.div(me, PAIR), lax.rem(me, PAIR)
    y_peer = {"fin": z * PAIR + (1 - y)}
    sibling = {"fout": 1 - core}

    def line_at(step):
        return lax.rem(z + step, lines)

    loads = []
    for part in range(parts):
        loads.append(pltpu.make_async_copy(wq.at[part], wq_v.at[part], wsem.at[part]))
    for g in range(groups):
        at = pl.ds(g * up_w, up_w)
        loads.append(pltpu.make_async_copy(wu.at[:, at], wu_v.at[:, at], wsem.at[parts + g]))
    base = parts + groups
    loads.append(pltpu.make_async_copy(wo, wo_v, wsem.at[base]))
    for j in range(chunks):
        at = pl.ds(j * out_w, out_w)
        loads.append(pltpu.make_async_copy(wd.at[:, at], wd_v.at[:, at], wsem.at[base + 1 + j]))
    for load in loads:
        load.start()

    barrier = pltpu.get_barrier_semaphore()
    pl.semaphore_signal(barrier, inc=1, device_id=y_peer, device_id_type=MESH)
    pl.semaphore_signal(barrier, inc=1, device_id=sibling, device_id_type=MESH)
    for step in range(1, lines):
        pl.semaphore_signal(
            barrier, inc=1, device_id={"fin": line_at(step) * PAIR + y}, device_id_type=MESH
        )

    values = tokens[...].astype(jnp.float32)
    center = jnp.mean(values, -1, keepdims=True)
    square = jnp.mean(values * values, -1, keepdims=True)
    scale = lax.rsqrt(square - center * center + 1e-06)
    mine = pl.ds(pl.multiple_of(core * half, LANES), half)
    normed = (tokens[:, mine].astype(jnp.float32) - center) * scale * gain[:, mine]
    fold = half // 2
    packed = jnp.concatenate([normed[:, :fold], normed[:, fold:]], axis=0)
    xg[me, :, pl.ds(0, fold)] = packed.astype(jnp.bfloat16)
    row = lax.broadcasted_iota(jnp.int32, (2 * rows, LANES), 0)
    mark = jnp.zeros((2 * rows, LANES), jnp.float32)
    for r in range(rows):
        mark = jnp.where(row == r, ids[r].astype(jnp.float32), mark)
    xg[me, :, pl.ds(fold, LANES)] = mark.astype(jnp.bfloat16)

    pl.semaphore_wait(barrier, lines + 1)

    def block(at, sem, to):
        return pltpu.make_async_remote_copy(
            src_ref=xg.at[at], dst_ref=xg.at[at], send_sem=gsend.at[sem], recv_sem=grecv.at[at],
            device_id=to, device_id_type=MESH,
        )

    sends = [block(me, 0, y_peer)]
    for step in range(1, lines):
        sends.append(block(me, step, {"fin": line_at(step) * PAIR + y}))
    for send in sends:
        send.start()
    for step in range(1, lines):
        source = line_at(lines - step) * PAIR + y
        passed = block(source, lines - 1 + step, y_peer)
        passed.wait_recv()
        passed.start()
        sends.append(passed)
    for step in range(lines):
        block(line_at(lines - step) * PAIR + (1 - y), 0, y_peer).wait_recv()

    for line in range(lines):
        pair = [xg[line * PAIR + k].astype(jnp.float32) for k in range(PAIR)]
        to = pl.ds(line * PAIR * rows, PAIR * rows)
        xs[to, pl.ds(0, fold)] = jnp.concatenate(
            [b[:rows, :fold] for b in pair], axis=0).astype(jnp.bfloat16)
        xs[to, pl.ds(fold, fold)] = jnp.concatenate(
            [b[rows:, :fold] for b in pair], axis=0).astype(jnp.bfloat16)
        idc[to, :] = jnp.concatenate([b[:rows, fold:] for b in pair], axis=0)

    swaps = []

    def project(g, weight, start, size):
        loads[g].wait()

        def tile(t, carry):
            src = pl.ds(pl.multiple_of(start + t * TILE, TILE), TILE)
            dst = pl.ds(pl.multiple_of(t * TILE, TILE), TILE)
            ps[g, :, dst] = jnp.dot(xs[...], weight[:, src], preferred_element_type=jnp.float32)
            return carry

        lax.fori_loop(0, size // TILE, tile, 0)
        swap = pltpu.make_async_remote_copy(
            src_ref=ps.at[g], dst_ref=pr.at[g], send_sem=psend.at[g], recv_sem=precv.at[g],
            device_id=sibling, device_id_type=MESH,
        )
        swap.start()
        swaps.append(swap)

    def activate(g):
        swaps[parts + g].wait_recv()
        total = ps[parts + g] + pr[parts + g]
        total = 0.5 * total * (1.0 + lax.erf(total * math.sqrt(0.5)))
        hid[:, pl.ds(g * up_w, up_w)] = total.astype(jnp.bfloat16)

    for part in range(parts):
        project(part, wq_v.at[part], 0, cols)
    for g in range(groups):
        project(parts + g, wu_v, g * up_w, up_w)
        if g:
            activate(g - 1)

    for part in range(parts):
        swaps[part].wait_recv()
    diagonal = lax.broadcasted_iota(jnp.int32, (toks, toks), 0) == lax.broadcasted_iota(
        jnp.int32, (toks, toks), 1)
    by_row = idc[:, pl.ds(0, toks)]
    same = by_row == jnp.sum(jnp.where(diagonal, by_row, 0.0), axis=0, keepdims=True)

    def head_norm(v):
        m = jnp.mean(v, -1, keepdims=True)
        s = jnp.mean(v * v, -1, keepdims=True)
        return ((v - m) * lax.rsqrt(s - m * m + 1e-06)).astype(jnp.bfloat16)

    for h in range(cols // HEAD):
        at = pl.ds(h * HEAD, HEAD)
        q, k, v = [(ps[i, :, at] + pr[i, :, at]).astype(jnp.bfloat16) for i in range(3)]
        qn, kn = head_norm(q.astype(jnp.float32)), head_norm(k.astype(jnp.float32))
        scores = lax.dot_general(
            qn, kn, (((1,), (1,)), ((), ())), preferred_element_type=jnp.float32
        ) * (1.0 / math.sqrt(HEAD))
        e = jnp.where(same, jnp.exp(scores), 0.0).astype(jnp.bfloat16)
        den = jnp.sum(e.astype(jnp.float32), -1, keepdims=True)
        total = jnp.dot(e, v, preferred_element_type=jnp.float32)
        att[:, at] = (total / den).astype(jnp.bfloat16)
    activate(groups - 1)

    loads[base].wait()
    reduces = []

    def line_rows(line, who):
        return pl.ds(pl.multiple_of(line * (PAIR * rows) + who * rows, rows), rows)

    def to_pair(j):
        at = pl.ds(j * out_w, out_w)
        theirs = jnp.concatenate([p[line_rows(k, 1 - y), at] for k in range(lines)], axis=0)
        ys[j] = theirs.astype(jnp.bfloat16)
        copy = pltpu.make_async_remote_copy(
            src_ref=ys.at[j], dst_ref=yr.at[j], send_sem=ysend.at[j], recv_sem=yrecv.at[j],
            device_id=y_peer, device_id_type=MESH,
        )
        copy.start()
        return copy

    def to_line(j, arrived):
        arrived.wait_recv()
        at = pl.ds(j * out_w, out_w)
        got = yr[j].astype(jnp.float32)
        for k in range(lines):
            total = p[line_rows(k, y), at] + got[k * rows:(k + 1) * rows]
            own[k, :, at] = total
            zs[j, k] = jnp.concatenate(
                [total[:, :out_w // 2], total[:, out_w // 2:]], axis=0).astype(jnp.bfloat16)
        copies = []
        for step in range(1, lines):
            line = line_at(step)
            copy = pltpu.make_async_remote_copy(
                src_ref=zs.at[j, line], dst_ref=zr.at[j, step - 1],
                send_sem=zsend.at[j, step - 1], recv_sem=zrecv.at[j, step - 1],
                device_id={"fin": line * PAIR + y}, device_id_type=MESH,
            )
            copy.start()
            copies.append(copy)
        reduces.append(copies)

    pairs = []
    for j in range(chunks):
        loads[base + 1 + j].wait()

        def tile(t, carry):
            at = pl.ds(pl.multiple_of(j * out_w + t * TILE, TILE), TILE)
            p[:, at] = jnp.dot(
                att[...], wo_v[:, at], preferred_element_type=jnp.float32
            ) + jnp.dot(hid[...], wd_v[:, at], preferred_element_type=jnp.float32)
            return carry

        lax.fori_loop(0, out_w // TILE, tile, 0)
        pairs.append(to_pair(j))
        if j:
            to_line(j - 1, pairs[j - 1])
    to_line(chunks - 1, pairs[chunks - 1])

    for j in range(chunks):
        at = pl.ds(j * out_w, out_w)
        total = own[z, :, at]
        for copy_at, copy in enumerate(reduces[j]):
            copy.wait_recv()
            got = zr[j, copy_at].astype(jnp.float32)
            total = total + jnp.concatenate([got[:rows], got[rows:]], axis=1)
        residual = tokens[:, pl.ds(pl.multiple_of(core * half + j * out_w, LANES), out_w)]
        out[:, at] = (residual.astype(jnp.float32) + total).astype(jnp.bfloat16)

    for copy in sends + swaps + pairs:
        copy.wait_send()
    for copies in reduces:
        for copy in copies:
            copy.wait_send()


def fused(lines, tokens, segment_ids, norm_gain, w_qkv, w_up, w_out, w_down):
    rows = tokens.shape[0]
    half, parts, cols = w_qkv.shape
    wide = w_up.shape[1]
    count = lines * PAIR
    toks = rows * count
    groups = wide // cols
    chunks = half // cols
    out_w = half // chunks
    bf16, f32 = jnp.bfloat16, jnp.float32
    dma = pltpu.SemaphoreType.DMA
    vmem = pl.BlockSpec(memory_space=pltpu.VMEM)
    hbm = pl.BlockSpec(memory_space=pl.ANY)
    macs = toks * (half * (parts * cols + wide) + (cols + wide) * half)
    return pl.pallas_call(
        functools.partial(fused_kernel, lines, groups, chunks),
        out_shape=jax.ShapeDtypeStruct((rows, half), bf16),
        in_specs=[vmem, pl.BlockSpec(memory_space=pltpu.SMEM), vmem, hbm, hbm, hbm, hbm],
        out_specs=vmem,
        scratch_shapes=[
            pltpu.VMEM((parts, half, cols), bf16),
            pltpu.VMEM((half, wide), bf16),
            pltpu.VMEM((cols, half), bf16),
            pltpu.VMEM((wide, half), bf16),
            pltpu.VMEM((count, 2 * rows, half // 2 + LANES), bf16),
            pltpu.VMEM((toks, half), bf16),
            pltpu.VMEM((toks, LANES), f32),
            pltpu.VMEM((parts + groups, toks, cols), f32),
            pltpu.VMEM((parts + groups, toks, cols), f32),
            pltpu.VMEM((toks, cols), bf16),
            pltpu.VMEM((toks, wide), bf16),
            pltpu.VMEM((toks, half), f32),
            pltpu.VMEM((chunks, toks // PAIR, out_w), bf16),
            pltpu.VMEM((chunks, toks // PAIR, out_w), bf16),
            pltpu.VMEM((chunks, lines, 2 * rows, out_w // 2), bf16),
            pltpu.VMEM((chunks, lines - 1, 2 * rows, out_w // 2), bf16),
            pltpu.VMEM((lines, rows, half), f32),
            dma((parts + groups + 1 + chunks,)),
            dma((2 * lines - 1,)),
            dma((count,)),
            dma((parts + groups,)),
            dma((parts + groups,)),
            dma((chunks,)),
            dma((chunks,)),
            dma((chunks, lines - 1)),
            dma((chunks, lines - 1)),
        ],
        compiler_params=pltpu.CompilerParams(
            collective_id=0, has_side_effects=True, vmem_limit_bytes=VMEM_LIMIT
        ),
        cost_estimate=pl.CostEstimate(
            flops=2 * macs, bytes_accessed=2 * macs // toks, transcendentals=0
        ),
    )(
        tokens, segment_ids, norm_gain.reshape(1, -1), jnp.transpose(w_qkv, (1, 0, 2)),
        w_up, w_out, w_down,
    )


VMEM_LIMIT = 63 << 20


def feature_norm(values):
    center = jnp.mean(values, -1, keepdims=True)
    square = jnp.mean(values * values, -1, keepdims=True)
    return (values - center) * lax.rsqrt(square - center * center + 1e-06)


def attend(qkv_local, query_ids):
    spread = lax.all_to_all(qkv_local, "fin", split_axis=0, concat_axis=2, tiled=True)
    spread = spread.reshape(spread.shape[0], 3, -1, HEAD)
    query = feature_norm(spread[:, 0].astype(jnp.float32)).astype(jnp.bfloat16)
    keys = feature_norm(spread[:, 1].astype(jnp.float32)).astype(jnp.bfloat16)
    value = spread[:, 2]
    tok_rows, heads, head_size = query.shape
    factor = 1.0 / math.sqrt(head_size)
    marks = query_ids + 1
    key_part = lax.all_gather(keys, "fin", axis=0, tiled=True)
    value_part = lax.all_gather(value, "fin", axis=0, tiled=True)
    mark_part = lax.all_gather(marks, "fin", axis=0, tiled=True)
    scores = (
        jnp.einsum("qhd,khd->hqk", query, key_part, preferred_element_type=jnp.float32) * factor
    )
    same = marks[:, None] == mark_part[None, :]
    weight = jnp.where(same[None], jnp.exp(scores), 0.0).astype(jnp.bfloat16)
    den = jnp.sum(weight.astype(jnp.float32), -1)
    total = jnp.einsum("hqk,khd->qhd", weight, value_part, preferred_element_type=jnp.float32)
    total, den = (total, den)
    attended = (total / jnp.transpose(den)[:, :, None]).astype(jnp.bfloat16)
    return attended.reshape(tok_rows, heads * head_size)


def local(tokens, segment_ids, norm_gain, w_qkv, w_up, w_out, w_down):
    values = tokens.astype(jnp.float32)
    normed_full = (feature_norm(values) * norm_gain).astype(jnp.bfloat16)
    half_width = w_qkv.shape[0]
    offset = lax.axis_index("fout") * half_width
    normed = lax.dynamic_slice_in_dim(normed_full, offset, half_width, 1)
    residual = lax.dynamic_slice_in_dim(values, offset, half_width, 1)
    parts, columns = (w_qkv.shape[1], w_qkv.shape[2])
    qkv_cols = parts * columns
    qkv_matrix = w_qkv.reshape(half_width, qkv_cols)
    piece = lax.all_gather(normed, "fin", axis=0, tiled=True)
    first = jnp.dot(piece, qkv_matrix, preferred_element_type=jnp.float32)
    second = jnp.dot(piece, w_up, preferred_element_type=jnp.float32)
    partial_value = jnp.concatenate([first, second], axis=1)
    qkv_part = partial_value[:, :qkv_cols].reshape(partial_value.shape[0], parts, columns)
    up_part = partial_value[:, qkv_cols:]
    qkv_sum, up_sum = lax.psum((qkv_part, up_part), "fout")
    attended = attend(qkv_sum.astype(jnp.bfloat16), segment_ids)
    hidden = jax.nn.gelu(up_sum, approximate=False).astype(jnp.bfloat16)
    head_block = lax.all_to_all(attended, "fin", split_axis=1, concat_axis=0, tiled=True)
    first = jnp.dot(head_block, w_out, preferred_element_type=jnp.float32)
    mixed = lax.psum_scatter(
        first + jnp.dot(hidden, w_down, preferred_element_type=jnp.float32),
        "fin",
        scatter_dimension=0,
        tiled=True,
    )
    return (residual + mixed).astype(jnp.bfloat16)


def fits(mesh, tokens, w_qkv, w_up, w_out):
    fin, rows = mesh.shape["fin"], tokens.shape[0] // (mesh.shape["grp"] * mesh.shape["fin"])
    half, cols = w_qkv.shape[0] // mesh.shape["fout"], w_qkv.shape[2] // fin
    wide = w_up.shape[1] // fin
    weights = 2 * half * (w_qkv.shape[1] * cols + cols + 2 * wide)
    return (
        mesh.shape["fout"] == 2 and fin % PAIR == 0 and fin > PAIR and rows == 8
        and rows * fin <= LANES and cols % TILE == 0 and cols % HEAD == 0
        and wide % cols == 0 and half % cols == 0 and weights <= 56 << 20
    )


def solution(mesh):
    def run(*args):
        tokens, _, _, w_qkv, w_up, w_out, _ = args
        if fits(mesh, tokens, w_qkv, w_up, w_out):
            body = functools.partial(fused, mesh.shape["fin"] // PAIR)
        else:
            body = local
        return placed(mesh, body)(*args)

    return run


def placed(mesh, body):
    return jax.shard_map(
        body,
        mesh=mesh,
        in_specs=(
            P(("grp", "fin"), None),
            P(("grp", "fin")),
            P(),
            P("fout", None, "fin"),
            P("fout", "fin"),
            P("fin", "fout"),
            P("fin", "fout"),
        ),
        out_specs=P(("grp", "fin"), "fout"),
        check_vma=False,
    )
```

```python
import functools
import math

import jax
import jax.numpy as jnp
from jax import lax
from jax.experimental import pallas as pl
from jax.experimental.pallas import tpu as pltpu
from jax.sharding import PartitionSpec as P

HEAD = 128
LANES = 128
TILE = 256
PAIR = 2
HALVES = 2
LAG = 2
MESH = pl.DeviceIdType.MESH


def fused_kernel(
    lines, groups, chunks,
    tokens, ids, gain, wq, wu, wo, wd, out,
    wq_v, wu_v, wo_v, wd_v, xa, xb, xs, idc, ps, pr, att, hid, p, ys, yr, zs, zr, own,
    wsem, gsend, grecv, psend, precv, ysend, yrecv, zsend, zrecv,
):
    rows, width = tokens.shape
    half = wu.shape[0]
    parts, _, cols = wq.shape
    count = lines * PAIR
    toks = rows * count
    up_w = wu.shape[1] // groups
    out_w = half // chunks
    me = lax.axis_index("fin")
    core = lax.axis_index("fout")
    z, y = lax.div(me, PAIR), lax.rem(me, PAIR)
    y_peer = {"fin": z * PAIR + (1 - y)}
    sibling = {"fout": 1 - core}

    def line_at(step):
        return lax.rem(z + step, lines)

    fold = half // HALVES
    columns = parts + groups
    loads = []
    for f in range(HALVES):
        depth = pl.ds(f * fold, fold)
        for part in range(parts):
            loads.append(pltpu.make_async_copy(
                wq.at[part, depth], wq_v.at[part, depth], wsem.at[f * columns + part]))
        for g in range(groups):
            at = pl.ds(g * up_w, up_w)
            loads.append(pltpu.make_async_copy(
                wu.at[depth, at], wu_v.at[depth, at], wsem.at[f * columns + parts + g]))
    base = HALVES * columns
    loads.append(pltpu.make_async_copy(wo, wo_v, wsem.at[base]))
    for j in range(chunks):
        at = pl.ds(j * out_w, out_w)
        loads.append(pltpu.make_async_copy(wd.at[:, at], wd_v.at[:, at], wsem.at[base + 1 + j]))
    for load in loads:
        load.start()

    barrier = pltpu.get_barrier_semaphore()
    pl.semaphore_signal(barrier, inc=1, device_id=y_peer, device_id_type=MESH)
    pl.semaphore_signal(barrier, inc=1, device_id=sibling, device_id_type=MESH)
    for step in range(1, lines):
        pl.semaphore_signal(
            barrier, inc=1, device_id={"fin": line_at(step) * PAIR + y}, device_id_type=MESH
        )

    values = tokens[...].astype(jnp.float32)
    center = jnp.mean(values, -1, keepdims=True)
    square = jnp.mean(values * values, -1, keepdims=True)
    scale = lax.rsqrt(square - center * center + 1e-06)
    mine = pl.ds(pl.multiple_of(core * half, LANES), half)
    normed = (tokens[:, mine].astype(jnp.float32) - center) * scale * gain[:, mine]
    piece = fold // 2
    blocks = (xa, xb)
    for f in range(HALVES):
        low = f * fold
        packed = jnp.concatenate(
            [normed[:, low:low + piece], normed[:, low + piece:low + fold]], axis=0)
        blocks[f][me, :, pl.ds(0, piece)] = packed.astype(jnp.bfloat16)
    row = lax.broadcasted_iota(jnp.int32, (2 * rows, LANES), 0)
    mark = jnp.zeros((2 * rows, LANES), jnp.float32)
    for r in range(rows):
        mark = jnp.where(row == r, ids[r].astype(jnp.float32), mark)
    xb[me, :, pl.ds(piece, LANES)] = mark.astype(jnp.bfloat16)

    pl.semaphore_wait(barrier, lines + 1)

    def block(f, at, sem, to):
        return pltpu.make_async_remote_copy(
            src_ref=blocks[f].at[at], dst_ref=blocks[f].at[at],
            send_sem=gsend.at[f, sem], recv_sem=grecv.at[f, at],
            device_id=to, device_id_type=MESH,
        )

    sends = []
    for f in range(HALVES):
        sends.append(block(f, me, 0, y_peer))
        for step in range(1, lines):
            sends.append(block(f, me, step, {"fin": line_at(step) * PAIR + y}))
    for send in sends:
        send.start()

    def pass_on(f, step):
        source = line_at(lines - step) * PAIR + y
        passed = block(f, source, lines - 1 + step, y_peer)
        passed.wait_recv()
        passed.start()
        sends.append(passed)

    def unpack(f):
        for step in range(lines):
            block(f, line_at(lines - step) * PAIR + (1 - y), 0, y_peer).wait_recv()
        low = f * fold
        for line in range(lines):
            pair = [blocks[f][line * PAIR + k].astype(jnp.float32) for k in range(PAIR)]
            to = pl.ds(line * PAIR * rows, PAIR * rows)
            xs[to, pl.ds(low, piece)] = jnp.concatenate(
                [b[:rows, :piece] for b in pair], axis=0).astype(jnp.bfloat16)
            xs[to, pl.ds(low + piece, piece)] = jnp.concatenate(
                [b[rows:, :piece] for b in pair], axis=0).astype(jnp.bfloat16)
            if f:
                idc[to, :] = jnp.concatenate([b[:rows, piece:] for b in pair], axis=0)

    for step in range(1, lines):
        pass_on(0, step)
    unpack(0)

    swaps = []

    def project(f, g, weight, start, size):
        loads[f * columns + g].wait()
        depth = pl.ds(f * fold, fold)

        def tile(t, carry):
            src = pl.ds(pl.multiple_of(start + t * TILE, TILE), TILE)
            dst = pl.ds(pl.multiple_of(t * TILE, TILE), TILE)
            product = jnp.dot(
                xs[:, depth], weight[depth, src], preferred_element_type=jnp.float32)
            ps[g, :, dst] = ps[g, :, dst] + product if f else product
            return carry

        lax.fori_loop(0, size // TILE, tile, 0)
        if f < HALVES - 1:
            return
        swap = pltpu.make_async_remote_copy(
            src_ref=ps.at[g], dst_ref=pr.at[g], send_sem=psend.at[g], recv_sem=precv.at[g],
            device_id=sibling, device_id_type=MESH,
        )
        swap.start()
        swaps.append(swap)

    def activate(g):
        swaps[parts + g].wait_recv()
        total = ps[parts + g] + pr[parts + g]
        total = 0.5 * total * (1.0 + lax.erf(total * math.sqrt(0.5)))
        hid[:, pl.ds(g * up_w, up_w)] = total.astype(jnp.bfloat16)

    def project_all(f, then):
        for part in range(parts):
            project(f, part, wq_v.at[part], 0, cols)
            then(part)
        for g in range(groups):
            project(f, parts + g, wu_v, g * up_w, up_w)
            then(parts + g)

    def between(at):
        if at % 2 == 0 and at // 2 + 1 < lines:
            pass_on(1, at // 2 + 1)

    def after(at):
        if at > parts:
            activate(at - parts - 1)

    project_all(0, between)
    for step in range(columns // 2 + columns % 2 + 1, lines):
        pass_on(1, step)
    unpack(1)
    project_all(1, after)

    for part in range(parts):
        swaps[part].wait_recv()
    diagonal = lax.broadcasted_iota(jnp.int32, (toks, toks), 0) == lax.broadcasted_iota(
        jnp.int32, (toks, toks), 1)
    by_row = idc[:, pl.ds(0, toks)]
    same = by_row == jnp.sum(jnp.where(diagonal, by_row, 0.0), axis=0, keepdims=True)

    def head_norm(v):
        m = jnp.mean(v, -1, keepdims=True)
        s = jnp.mean(v * v, -1, keepdims=True)
        return ((v - m) * lax.rsqrt(s - m * m + 1e-06)).astype(jnp.bfloat16)

    for h in range(cols // HEAD):
        at = pl.ds(h * HEAD, HEAD)
        q, k, v = [(ps[i, :, at] + pr[i, :, at]).astype(jnp.bfloat16) for i in range(3)]
        qn, kn = head_norm(q.astype(jnp.float32)), head_norm(k.astype(jnp.float32))
        scores = lax.dot_general(
            qn, kn, (((1,), (1,)), ((), ())), preferred_element_type=jnp.float32
        ) * (1.0 / math.sqrt(HEAD))
        e = jnp.where(same, jnp.exp(scores), 0.0).astype(jnp.bfloat16)
        den = jnp.sum(e.astype(jnp.float32), -1, keepdims=True)
        total = jnp.dot(e, v, preferred_element_type=jnp.float32)
        att[:, at] = (total / den).astype(jnp.bfloat16)
    activate(groups - 1)

    loads[base].wait()
    reduces = []

    def line_rows(line, who):
        return pl.ds(pl.multiple_of(line * (PAIR * rows) + who * rows, rows), rows)

    def to_pair(j):
        at = pl.ds(j * out_w, out_w)
        theirs = jnp.concatenate([p[line_rows(k, 1 - y), at] for k in range(lines)], axis=0)
        ys[j] = theirs.astype(jnp.bfloat16)
        copy = pltpu.make_async_remote_copy(
            src_ref=ys.at[j], dst_ref=yr.at[j], send_sem=ysend.at[j], recv_sem=yrecv.at[j],
            device_id=y_peer, device_id_type=MESH,
        )
        copy.start()
        return copy

    def to_line(j, arrived):
        arrived.wait_recv()
        at = pl.ds(j * out_w, out_w)
        got = yr[j].astype(jnp.float32)
        for k in range(lines):
            total = p[line_rows(k, y), at] + got[k * rows:(k + 1) * rows]
            own[k, :, at] = total
            zs[j, k] = jnp.concatenate(
                [total[:, :out_w // 2], total[:, out_w // 2:]], axis=0).astype(jnp.bfloat16)
        copies = []
        for step in range(1, lines):
            line = line_at(step)
            copy = pltpu.make_async_remote_copy(
                src_ref=zs.at[j, line], dst_ref=zr.at[j, step - 1],
                send_sem=zsend.at[j, step - 1], recv_sem=zrecv.at[j, step - 1],
                device_id={"fin": line * PAIR + y}, device_id_type=MESH,
            )
            copy.start()
            copies.append(copy)
        reduces.append(copies)

    pairs = []
    for j in range(chunks):
        loads[base + 1 + j].wait()

        def tile(t, carry):
            at = pl.ds(pl.multiple_of(j * out_w + t * TILE, TILE), TILE)
            p[:, at] = jnp.dot(
                att[...], wo_v[:, at], preferred_element_type=jnp.float32
            ) + jnp.dot(hid[...], wd_v[:, at], preferred_element_type=jnp.float32)
            return carry

        lax.fori_loop(0, out_w // TILE, tile, 0)
        pairs.append(to_pair(j))
        if j >= LAG:
            to_line(j - LAG, pairs[j - LAG])
    for j in range(chunks - LAG, chunks):
        to_line(j, pairs[j])

    for j in range(chunks):
        at = pl.ds(j * out_w, out_w)
        total = own[z, :, at]
        for copy_at, copy in enumerate(reduces[j]):
            copy.wait_recv()
            got = zr[j, copy_at].astype(jnp.float32)
            total = total + jnp.concatenate([got[:rows], got[rows:]], axis=1)
        residual = tokens[:, pl.ds(pl.multiple_of(core * half + j * out_w, LANES), out_w)]
        out[:, at] = (residual.astype(jnp.float32) + total).astype(jnp.bfloat16)

    for copy in sends + swaps + pairs:
        copy.wait_send()
    for copies in reduces:
        for copy in copies:
            copy.wait_send()


def fused(lines, tokens, segment_ids, norm_gain, w_qkv, w_up, w_out, w_down):
    rows = tokens.shape[0]
    half, parts, cols = w_qkv.shape
    wide = w_up.shape[1]
    count = lines * PAIR
    toks = rows * count
    groups = wide // cols
    chunks = half // (2 * TILE)
    out_w = half // chunks
    bf16, f32 = jnp.bfloat16, jnp.float32
    dma = pltpu.SemaphoreType.DMA
    vmem = pl.BlockSpec(memory_space=pltpu.VMEM)
    hbm = pl.BlockSpec(memory_space=pl.ANY)
    macs = toks * (half * (parts * cols + wide) + (cols + wide) * half)
    return pl.pallas_call(
        functools.partial(fused_kernel, lines, groups, chunks),
        out_shape=jax.ShapeDtypeStruct((rows, half), bf16),
        in_specs=[vmem, pl.BlockSpec(memory_space=pltpu.SMEM), vmem, hbm, hbm, hbm, hbm],
        out_specs=vmem,
        scratch_shapes=[
            pltpu.VMEM((parts, half, cols), bf16),
            pltpu.VMEM((half, wide), bf16),
            pltpu.VMEM((cols, half), bf16),
            pltpu.VMEM((wide, half), bf16),
            pltpu.VMEM((count, 2 * rows, half // 4), bf16),
            pltpu.VMEM((count, 2 * rows, half // 4 + LANES), bf16),
            pltpu.VMEM((toks, half), bf16),
            pltpu.VMEM((toks, LANES), f32),
            pltpu.VMEM((parts + groups, toks, cols), f32),
            pltpu.VMEM((parts + groups, toks, cols), f32),
            pltpu.VMEM((toks, cols), bf16),
            pltpu.VMEM((toks, wide), bf16),
            pltpu.VMEM((toks, half), f32),
            pltpu.VMEM((chunks, toks // PAIR, out_w), bf16),
            pltpu.VMEM((chunks, toks // PAIR, out_w), bf16),
            pltpu.VMEM((chunks, lines, 2 * rows, out_w // 2), bf16),
            pltpu.VMEM((chunks, lines - 1, 2 * rows, out_w // 2), bf16),
            pltpu.VMEM((lines, rows, half), f32),
            dma((HALVES * (parts + groups) + 1 + chunks,)),
            dma((HALVES, 2 * lines - 1)),
            dma((HALVES, count)),
            dma((parts + groups,)),
            dma((parts + groups,)),
            dma((chunks,)),
            dma((chunks,)),
            dma((chunks, lines - 1)),
            dma((chunks, lines - 1)),
        ],
        compiler_params=pltpu.CompilerParams(
            collective_id=0, has_side_effects=True, vmem_limit_bytes=VMEM_LIMIT
        ),
        cost_estimate=pl.CostEstimate(
            flops=2 * macs, bytes_accessed=2 * macs // toks, transcendentals=0
        ),
    )(
        tokens, segment_ids, norm_gain.reshape(1, -1), jnp.transpose(w_qkv, (1, 0, 2)),
        w_up, w_out, w_down,
    )


VMEM_LIMIT = 63 << 20


def feature_norm(values):
    center = jnp.mean(values, -1, keepdims=True)
    square = jnp.mean(values * values, -1, keepdims=True)
    return (values - center) * lax.rsqrt(square - center * center + 1e-06)


def attend(qkv_local, query_ids):
    spread = lax.all_to_all(qkv_local, "fin", split_axis=0, concat_axis=2, tiled=True)
    spread = spread.reshape(spread.shape[0], 3, -1, HEAD)
    query = feature_norm(spread[:, 0].astype(jnp.float32)).astype(jnp.bfloat16)
    keys = feature_norm(spread[:, 1].astype(jnp.float32)).astype(jnp.bfloat16)
    value = spread[:, 2]
    tok_rows, heads, head_size = query.shape
    factor = 1.0 / math.sqrt(head_size)
    marks = query_ids + 1
    key_part = lax.all_gather(keys, "fin", axis=0, tiled=True)
    value_part = lax.all_gather(value, "fin", axis=0, tiled=True)
    mark_part = lax.all_gather(marks, "fin", axis=0, tiled=True)
    scores = (
        jnp.einsum("qhd,khd->hqk", query, key_part, preferred_element_type=jnp.float32) * factor
    )
    same = marks[:, None] == mark_part[None, :]
    weight = jnp.where(same[None], jnp.exp(scores), 0.0).astype(jnp.bfloat16)
    den = jnp.sum(weight.astype(jnp.float32), -1)
    total = jnp.einsum("hqk,khd->qhd", weight, value_part, preferred_element_type=jnp.float32)
    total, den = (total, den)
    attended = (total / jnp.transpose(den)[:, :, None]).astype(jnp.bfloat16)
    return attended.reshape(tok_rows, heads * head_size)


def local(tokens, segment_ids, norm_gain, w_qkv, w_up, w_out, w_down):
    values = tokens.astype(jnp.float32)
    normed_full = (feature_norm(values) * norm_gain).astype(jnp.bfloat16)
    half_width = w_qkv.shape[0]
    offset = lax.axis_index("fout") * half_width
    normed = lax.dynamic_slice_in_dim(normed_full, offset, half_width, 1)
    residual = lax.dynamic_slice_in_dim(values, offset, half_width, 1)
    parts, columns = (w_qkv.shape[1], w_qkv.shape[2])
    qkv_cols = parts * columns
    qkv_matrix = w_qkv.reshape(half_width, qkv_cols)
    piece = lax.all_gather(normed, "fin", axis=0, tiled=True)
    first = jnp.dot(piece, qkv_matrix, preferred_element_type=jnp.float32)
    second = jnp.dot(piece, w_up, preferred_element_type=jnp.float32)
    partial_value = jnp.concatenate([first, second], axis=1)
    qkv_part = partial_value[:, :qkv_cols].reshape(partial_value.shape[0], parts, columns)
    up_part = partial_value[:, qkv_cols:]
    qkv_sum, up_sum = lax.psum((qkv_part, up_part), "fout")
    attended = attend(qkv_sum.astype(jnp.bfloat16), segment_ids)
    hidden = jax.nn.gelu(up_sum, approximate=False).astype(jnp.bfloat16)
    head_block = lax.all_to_all(attended, "fin", split_axis=1, concat_axis=0, tiled=True)
    first = jnp.dot(head_block, w_out, preferred_element_type=jnp.float32)
    mixed = lax.psum_scatter(
        first + jnp.dot(hidden, w_down, preferred_element_type=jnp.float32),
        "fin",
        scatter_dimension=0,
        tiled=True,
    )
    return (residual + mixed).astype(jnp.bfloat16)


def fits(mesh, tokens, w_qkv, w_up, w_out):
    fin, rows = mesh.shape["fin"], tokens.shape[0] // (mesh.shape["grp"] * mesh.shape["fin"])
    half, cols = w_qkv.shape[0] // mesh.shape["fout"], w_qkv.shape[2] // fin
    wide = w_up.shape[1] // fin
    weights = 2 * half * (w_qkv.shape[1] * cols + cols + 2 * wide)
    return (
        mesh.shape["fout"] == 2 and fin % PAIR == 0 and fin > PAIR and rows == 8
        and rows * fin <= LANES and cols % TILE == 0 and cols % HEAD == 0
        and wide % cols == 0 and half % (2 * LAG * TILE) == 0 and weights <= 56 << 20
    )


def solution(mesh):
    def run(*args):
        tokens, _, _, w_qkv, w_up, w_out, _ = args
        if fits(mesh, tokens, w_qkv, w_up, w_out):
            body = functools.partial(fused, mesh.shape["fin"] // PAIR)
        else:
            body = local
        return placed(mesh, body)(*args)

    return run


def placed(mesh, body):
    return jax.shard_map(
        body,
        mesh=mesh,
        in_specs=(
            P(("grp", "fin"), None),
            P(("grp", "fin")),
            P(),
            P("fout", None, "fin"),
            P("fout", "fin"),
            P("fin", "fout"),
            P("fin", "fout"),
        ),
        out_specs=P(("grp", "fin"), "fout"),
        check_vma=False,
    )
```

```python
import functools
import math

import jax
import jax.numpy as jnp
from jax import lax
from jax.experimental import pallas as pl
from jax.experimental.pallas import tpu as pltpu
from jax.sharding import PartitionSpec as P

HEAD = 128
LANES = 128
TILE = 256
PAIR = 2
LAG = 2
MESH = pl.DeviceIdType.MESH


def fused_kernel(
    lines, groups, chunks,
    tokens, ids, gain, wq, wu, wo, wd, out,
    wq_v, wu_v, wo_v, wd_v, xg, xs, idc, ps, pr, att, hid, p, ys, yr, zs, zr, own,
    wsem, gsend, grecv, psend, precv, ysend, yrecv, zsend, zrecv,
):
    rows, width = tokens.shape
    half = wu.shape[0]
    parts, _, cols = wq.shape
    count = lines * PAIR
    toks = rows * count
    up_w = wu.shape[1] // groups
    out_w = half // chunks
    me = lax.axis_index("fin")
    core = lax.axis_index("fout")
    z, y = lax.div(me, PAIR), lax.rem(me, PAIR)
    y_peer = {"fin": z * PAIR + (1 - y)}
    sibling = {"fout": 1 - core}

    def line_at(step):
        return lax.rem(z + step, lines)

    loads = []
    for part in range(parts):
        loads.append(pltpu.make_async_copy(wq.at[part], wq_v.at[part], wsem.at[part]))
    for g in range(groups):
        at = pl.ds(g * up_w, up_w)
        loads.append(pltpu.make_async_copy(wu.at[:, at], wu_v.at[:, at], wsem.at[parts + g]))
    base = parts + groups
    loads.append(pltpu.make_async_copy(wo, wo_v, wsem.at[base]))
    for j in range(chunks):
        at = pl.ds(j * out_w, out_w)
        loads.append(pltpu.make_async_copy(wd.at[:, at], wd_v.at[:, at], wsem.at[base + 1 + j]))
    for load in loads:
        load.start()

    barrier = pltpu.get_barrier_semaphore()
    pl.semaphore_signal(barrier, inc=1, device_id=y_peer, device_id_type=MESH)
    pl.semaphore_signal(barrier, inc=1, device_id=sibling, device_id_type=MESH)
    for step in range(1, lines):
        pl.semaphore_signal(
            barrier, inc=1, device_id={"fin": line_at(step) * PAIR + y}, device_id_type=MESH
        )

    values = tokens[...].astype(jnp.float32)
    center = jnp.mean(values, -1, keepdims=True)
    square = jnp.mean(values * values, -1, keepdims=True)
    scale = lax.rsqrt(square - center * center + 1e-06)
    mine = pl.ds(pl.multiple_of(core * half, LANES), half)
    normed = (tokens[:, mine].astype(jnp.float32) - center) * scale * gain[:, mine]
    fold = half // 2
    packed = jnp.concatenate([normed[:, :fold], normed[:, fold:]], axis=0)
    xg[me, :, pl.ds(0, fold)] = packed.astype(jnp.bfloat16)
    row = lax.broadcasted_iota(jnp.int32, (2 * rows, LANES), 0)
    mark = jnp.zeros((2 * rows, LANES), jnp.float32)
    for r in range(rows):
        mark = jnp.where(row == r, ids[r].astype(jnp.float32), mark)
    xg[me, :, pl.ds(fold, LANES)] = mark.astype(jnp.bfloat16)

    pl.semaphore_wait(barrier, lines + 1)

    def block(at, sem, to):
        return pltpu.make_async_remote_copy(
            src_ref=xg.at[at], dst_ref=xg.at[at], send_sem=gsend.at[sem], recv_sem=grecv.at[at],
            device_id=to, device_id_type=MESH,
        )

    sends = [block(me, 0, y_peer)]
    for step in range(1, lines):
        sends.append(block(me, step, {"fin": line_at(step) * PAIR + y}))
    for send in sends:
        send.start()
    for step in range(1, lines):
        source = line_at(lines - step) * PAIR + y
        passed = block(source, lines - 1 + step, y_peer)
        passed.wait_recv()
        passed.start()
        sends.append(passed)
    for step in range(lines):
        block(line_at(lines - step) * PAIR + (1 - y), 0, y_peer).wait_recv()

    for line in range(lines):
        pair = [xg[line * PAIR + k].astype(jnp.float32) for k in range(PAIR)]
        to = pl.ds(line * PAIR * rows, PAIR * rows)
        xs[to, pl.ds(0, fold)] = jnp.concatenate(
            [b[:rows, :fold] for b in pair], axis=0).astype(jnp.bfloat16)
        xs[to, pl.ds(fold, fold)] = jnp.concatenate(
            [b[rows:, :fold] for b in pair], axis=0).astype(jnp.bfloat16)
        idc[to, :] = jnp.concatenate([b[:rows, fold:] for b in pair], axis=0)

    swaps = []

    def project(g, weight, start, size):
        loads[g].wait()

        def tile(t, carry):
            src = pl.ds(pl.multiple_of(start + t * TILE, TILE), TILE)
            dst = pl.ds(pl.multiple_of(t * TILE, TILE), TILE)
            ps[g, :, dst] = jnp.dot(xs[...], weight[:, src], preferred_element_type=jnp.float32)
            return carry

        lax.fori_loop(0, size // TILE, tile, 0)
        swap = pltpu.make_async_remote_copy(
            src_ref=ps.at[g], dst_ref=pr.at[g], send_sem=psend.at[g], recv_sem=precv.at[g],
            device_id=sibling, device_id_type=MESH,
        )
        swap.start()
        swaps.append(swap)

    def activate(g):
        swaps[parts + g].wait_recv()
        total = ps[parts + g] + pr[parts + g]
        total = 0.5 * total * (1.0 + lax.erf(total * math.sqrt(0.5)))
        hid[:, pl.ds(g * up_w, up_w)] = total.astype(jnp.bfloat16)

    for part in range(parts):
        project(part, wq_v.at[part], 0, cols)
    for g in range(groups):
        project(parts + g, wu_v, g * up_w, up_w)
        if g:
            activate(g - 1)

    for part in range(parts):
        swaps[part].wait_recv()
    diagonal = lax.broadcasted_iota(jnp.int32, (toks, toks), 0) == lax.broadcasted_iota(
        jnp.int32, (toks, toks), 1)
    by_row = idc[:, pl.ds(0, toks)]
    same = by_row == jnp.sum(jnp.where(diagonal, by_row, 0.0), axis=0, keepdims=True)

    def head_norm(v):
        m = jnp.mean(v, -1, keepdims=True)
        s = jnp.mean(v * v, -1, keepdims=True)
        return ((v - m) * lax.rsqrt(s - m * m + 1e-06)).astype(jnp.bfloat16)

    for h in range(cols // HEAD):
        at = pl.ds(h * HEAD, HEAD)
        q, k, v = [(ps[i, :, at] + pr[i, :, at]).astype(jnp.bfloat16) for i in range(3)]
        qn, kn = head_norm(q.astype(jnp.float32)), head_norm(k.astype(jnp.float32))
        scores = lax.dot_general(
            qn, kn, (((1,), (1,)), ((), ())), preferred_element_type=jnp.float32
        ) * (1.0 / math.sqrt(HEAD))
        e = jnp.where(same, jnp.exp(scores), 0.0).astype(jnp.bfloat16)
        den = jnp.sum(e.astype(jnp.float32), -1, keepdims=True)
        total = jnp.dot(e, v, preferred_element_type=jnp.float32)
        att[:, at] = (total / den).astype(jnp.bfloat16)
    activate(groups - 1)

    loads[base].wait()
    reduces = []

    def line_rows(line, who):
        return pl.ds(pl.multiple_of(line * (PAIR * rows) + who * rows, rows), rows)

    def to_pair(j):
        at = pl.ds(j * out_w, out_w)
        theirs = jnp.concatenate([p[line_rows(k, 1 - y), at] for k in range(lines)], axis=0)
        ys[j] = theirs.astype(jnp.bfloat16)
        copy = pltpu.make_async_remote_copy(
            src_ref=ys.at[j], dst_ref=yr.at[j], send_sem=ysend.at[j], recv_sem=yrecv.at[j],
            device_id=y_peer, device_id_type=MESH,
        )
        copy.start()
        return copy

    def to_line(j, arrived):
        arrived.wait_recv()
        at = pl.ds(j * out_w, out_w)
        got = yr[j].astype(jnp.float32)
        for k in range(lines):
            total = p[line_rows(k, y), at] + got[k * rows:(k + 1) * rows]
            own[k, :, at] = total
            zs[j, k] = jnp.concatenate(
                [total[:, :out_w // 2], total[:, out_w // 2:]], axis=0).astype(jnp.bfloat16)
        copies = []
        for step in range(1, lines):
            line = line_at(step)
            copy = pltpu.make_async_remote_copy(
                src_ref=zs.at[j, line], dst_ref=zr.at[j, step - 1],
                send_sem=zsend.at[j, step - 1], recv_sem=zrecv.at[j, step - 1],
                device_id={"fin": line * PAIR + y}, device_id_type=MESH,
            )
            copy.start()
            copies.append(copy)
        reduces.append(copies)

    pairs = []
    for j in range(chunks):
        loads[base + 1 + j].wait()

        def tile(t, carry):
            at = pl.ds(pl.multiple_of(j * out_w + t * TILE, TILE), TILE)
            p[:, at] = jnp.dot(
                att[...], wo_v[:, at], preferred_element_type=jnp.float32
            ) + jnp.dot(hid[...], wd_v[:, at], preferred_element_type=jnp.float32)
            return carry

        lax.fori_loop(0, out_w // TILE, tile, 0)
        pairs.append(to_pair(j))
        if j >= LAG:
            to_line(j - LAG, pairs[j - LAG])
    for j in range(chunks - LAG, chunks):
        to_line(j, pairs[j])

    for j in range(chunks):
        at = pl.ds(j * out_w, out_w)
        total = own[z, :, at]
        for copy_at, copy in enumerate(reduces[j]):
            copy.wait_recv()
            got = zr[j, copy_at].astype(jnp.float32)
            total = total + jnp.concatenate([got[:rows], got[rows:]], axis=1)
        residual = tokens[:, pl.ds(pl.multiple_of(core * half + j * out_w, LANES), out_w)]
        out[:, at] = (residual.astype(jnp.float32) + total).astype(jnp.bfloat16)

    for copy in sends + swaps + pairs:
        copy.wait_send()
    for copies in reduces:
        for copy in copies:
            copy.wait_send()


def fused(lines, tokens, segment_ids, norm_gain, w_qkv, w_up, w_out, w_down):
    rows = tokens.shape[0]
    half, parts, cols = w_qkv.shape
    wide = w_up.shape[1]
    count = lines * PAIR
    toks = rows * count
    groups = wide // cols
    chunks = half // cols
    out_w = half // chunks
    bf16, f32 = jnp.bfloat16, jnp.float32
    dma = pltpu.SemaphoreType.DMA
    vmem = pl.BlockSpec(memory_space=pltpu.VMEM)
    hbm = pl.BlockSpec(memory_space=pl.ANY)
    macs = toks * (half * (parts * cols + wide) + (cols + wide) * half)
    return pl.pallas_call(
        functools.partial(fused_kernel, lines, groups, chunks),
        out_shape=jax.ShapeDtypeStruct((rows, half), bf16),
        in_specs=[vmem, pl.BlockSpec(memory_space=pltpu.SMEM), vmem, hbm, hbm, hbm, hbm],
        out_specs=vmem,
        scratch_shapes=[
            pltpu.VMEM((parts, half, cols), bf16),
            pltpu.VMEM((half, wide), bf16),
            pltpu.VMEM((cols, half), bf16),
            pltpu.VMEM((wide, half), bf16),
            pltpu.VMEM((count, 2 * rows, half // 2 + LANES), bf16),
            pltpu.VMEM((toks, half), bf16),
            pltpu.VMEM((toks, LANES), f32),
            pltpu.VMEM((parts + groups, toks, cols), f32),
            pltpu.VMEM((parts + groups, toks, cols), f32),
            pltpu.VMEM((toks, cols), bf16),
            pltpu.VMEM((toks, wide), bf16),
            pltpu.VMEM((toks, half), f32),
            pltpu.VMEM((chunks, toks // PAIR, out_w), bf16),
            pltpu.VMEM((chunks, toks // PAIR, out_w), bf16),
            pltpu.VMEM((chunks, lines, 2 * rows, out_w // 2), bf16),
            pltpu.VMEM((chunks, lines - 1, 2 * rows, out_w // 2), bf16),
            pltpu.VMEM((lines, rows, half), f32),
            dma((parts + groups + 1 + chunks,)),
            dma((2 * lines - 1,)),
            dma((count,)),
            dma((parts + groups,)),
            dma((parts + groups,)),
            dma((chunks,)),
            dma((chunks,)),
            dma((chunks, lines - 1)),
            dma((chunks, lines - 1)),
        ],
        compiler_params=pltpu.CompilerParams(
            collective_id=0, has_side_effects=True, vmem_limit_bytes=VMEM_LIMIT
        ),
        cost_estimate=pl.CostEstimate(
            flops=2 * macs, bytes_accessed=2 * macs // toks, transcendentals=0
        ),
    )(
        tokens, segment_ids, norm_gain.reshape(1, -1), jnp.transpose(w_qkv, (1, 0, 2)),
        w_up, w_out, w_down,
    )


VMEM_LIMIT = 63 << 20


def feature_norm(values):
    center = jnp.mean(values, -1, keepdims=True)
    square = jnp.mean(values * values, -1, keepdims=True)
    return (values - center) * lax.rsqrt(square - center * center + 1e-06)


def attend(qkv_local, query_ids):
    spread = lax.all_to_all(qkv_local, "fin", split_axis=0, concat_axis=2, tiled=True)
    spread = spread.reshape(spread.shape[0], 3, -1, HEAD)
    query = feature_norm(spread[:, 0].astype(jnp.float32)).astype(jnp.bfloat16)
    keys = feature_norm(spread[:, 1].astype(jnp.float32)).astype(jnp.bfloat16)
    value = spread[:, 2]
    tok_rows, heads, head_size = query.shape
    factor = 1.0 / math.sqrt(head_size)
    marks = query_ids + 1
    key_part = lax.all_gather(keys, "fin", axis=0, tiled=True)
    value_part = lax.all_gather(value, "fin", axis=0, tiled=True)
    mark_part = lax.all_gather(marks, "fin", axis=0, tiled=True)
    scores = (
        jnp.einsum("qhd,khd->hqk", query, key_part, preferred_element_type=jnp.float32) * factor
    )
    same = marks[:, None] == mark_part[None, :]
    weight = jnp.where(same[None], jnp.exp(scores), 0.0).astype(jnp.bfloat16)
    den = jnp.sum(weight.astype(jnp.float32), -1)
    total = jnp.einsum("hqk,khd->qhd", weight, value_part, preferred_element_type=jnp.float32)
    total, den = (total, den)
    attended = (total / jnp.transpose(den)[:, :, None]).astype(jnp.bfloat16)
    return attended.reshape(tok_rows, heads * head_size)


def local(tokens, segment_ids, norm_gain, w_qkv, w_up, w_out, w_down):
    values = tokens.astype(jnp.float32)
    normed_full = (feature_norm(values) * norm_gain).astype(jnp.bfloat16)
    half_width = w_qkv.shape[0]
    offset = lax.axis_index("fout") * half_width
    normed = lax.dynamic_slice_in_dim(normed_full, offset, half_width, 1)
    residual = lax.dynamic_slice_in_dim(values, offset, half_width, 1)
    parts, columns = (w_qkv.shape[1], w_qkv.shape[2])
    qkv_cols = parts * columns
    qkv_matrix = w_qkv.reshape(half_width, qkv_cols)
    piece = lax.all_gather(normed, "fin", axis=0, tiled=True)
    first = jnp.dot(piece, qkv_matrix, preferred_element_type=jnp.float32)
    second = jnp.dot(piece, w_up, preferred_element_type=jnp.float32)
    partial_value = jnp.concatenate([first, second], axis=1)
    qkv_part = partial_value[:, :qkv_cols].reshape(partial_value.shape[0], parts, columns)
    up_part = partial_value[:, qkv_cols:]
    qkv_sum, up_sum = lax.psum((qkv_part, up_part), "fout")
    attended = attend(qkv_sum.astype(jnp.bfloat16), segment_ids)
    hidden = jax.nn.gelu(up_sum, approximate=False).astype(jnp.bfloat16)
    head_block = lax.all_to_all(attended, "fin", split_axis=1, concat_axis=0, tiled=True)
    first = jnp.dot(head_block, w_out, preferred_element_type=jnp.float32)
    mixed = lax.psum_scatter(
        first + jnp.dot(hidden, w_down, preferred_element_type=jnp.float32),
        "fin",
        scatter_dimension=0,
        tiled=True,
    )
    return (residual + mixed).astype(jnp.bfloat16)


def fits(mesh, tokens, w_qkv, w_up, w_out):
    fin, rows = mesh.shape["fin"], tokens.shape[0] // (mesh.shape["grp"] * mesh.shape["fin"])
    half, cols = w_qkv.shape[0] // mesh.shape["fout"], w_qkv.shape[2] // fin
    wide = w_up.shape[1] // fin
    weights = 2 * half * (w_qkv.shape[1] * cols + cols + 2 * wide)
    return (
        mesh.shape["fout"] == 2 and fin % PAIR == 0 and fin > PAIR and rows == 8
        and rows * fin <= LANES and cols % TILE == 0 and cols % HEAD == 0
        and wide % cols == 0 and half % cols == 0 and half // cols >= LAG and weights <= 56 << 20
    )


def solution(mesh):
    def run(*args):
        tokens, _, _, w_qkv, w_up, w_out, _ = args
        if fits(mesh, tokens, w_qkv, w_up, w_out):
            body = functools.partial(fused, mesh.shape["fin"] // PAIR)
        else:
            body = local
        return placed(mesh, body)(*args)

    return run


def placed(mesh, body):
    return jax.shard_map(
        body,
        mesh=mesh,
        in_specs=(
            P(("grp", "fin"), None),
            P(("grp", "fin")),
            P(),
            P("fout", None, "fin"),
            P("fout", "fin"),
            P("fin", "fout"),
            P("fin", "fout"),
        ),
        out_specs=P(("grp", "fin"), "fout"),
        check_vma=False,
    )
```

```python
import functools
import math

import jax
import jax.numpy as jnp
from jax import lax
from jax.experimental import pallas as pl
from jax.experimental.pallas import tpu as pltpu
from jax.sharding import PartitionSpec as P

HEAD = 128
LANES = 128
TILE = 256
PAIR = 2
LAG = 2
MESH = pl.DeviceIdType.MESH


def fused_kernel(
    lines, groups, chunks,
    tokens, ids, gain, wq, wu, wo, wd, out,
    wq_v, wu_v, wo_v, wd_v, xg, xs, idc, ps, pr, att, hid, p, ys, yr, zs, zr, own,
    wsem, gsend, grecv, psend, precv, ysend, yrecv, zsend, zrecv,
):
    rows, width = tokens.shape
    half = wu.shape[0]
    parts, _, cols = wq.shape
    count = lines * PAIR
    toks = rows * count
    up_w = wu.shape[1] // groups
    out_w = half // chunks
    me = lax.axis_index("fin")
    core = lax.axis_index("fout")
    z, y = lax.div(me, PAIR), lax.rem(me, PAIR)
    y_peer = {"fin": z * PAIR + (1 - y)}
    sibling = {"fout": 1 - core}

    def line_at(step):
        return lax.rem(z + step, lines)

    loads = []
    for part in range(parts):
        loads.append(pltpu.make_async_copy(wq.at[part], wq_v.at[part], wsem.at[part]))
    for g in range(groups):
        at = pl.ds(g * up_w, up_w)
        loads.append(pltpu.make_async_copy(wu.at[:, at], wu_v.at[:, at], wsem.at[parts + g]))
    base = parts + groups
    loads.append(pltpu.make_async_copy(wo, wo_v, wsem.at[base]))
    for j in range(chunks):
        at = pl.ds(j * out_w, out_w)
        loads.append(pltpu.make_async_copy(wd.at[:, at], wd_v.at[:, at], wsem.at[base + 1 + j]))
    for load in loads:
        load.start()

    barrier = pltpu.get_barrier_semaphore()
    pl.semaphore_signal(barrier, inc=1, device_id=y_peer, device_id_type=MESH)
    pl.semaphore_signal(barrier, inc=1, device_id=sibling, device_id_type=MESH)
    for step in range(1, lines):
        pl.semaphore_signal(
            barrier, inc=1, device_id={"fin": line_at(step) * PAIR + y}, device_id_type=MESH
        )

    values = tokens[...].astype(jnp.float32)
    center = jnp.mean(values, -1, keepdims=True)
    square = jnp.mean(values * values, -1, keepdims=True)
    scale = lax.rsqrt(square - center * center + 1e-06)
    mine = pl.ds(pl.multiple_of(core * half, LANES), half)
    normed = (tokens[:, mine].astype(jnp.float32) - center) * scale * gain[:, mine]
    fold = half // 2
    packed = jnp.concatenate([normed[:, :fold], normed[:, fold:]], axis=0)
    xg[me, :, pl.ds(0, fold)] = packed.astype(jnp.bfloat16)
    row = lax.broadcasted_iota(jnp.int32, (2 * rows, LANES), 0)
    mark = jnp.zeros((2 * rows, LANES), jnp.float32)
    for r in range(rows):
        mark = jnp.where(row == r, ids[r].astype(jnp.float32), mark)
    xg[me, :, pl.ds(fold, LANES)] = mark.astype(jnp.bfloat16)

    pl.semaphore_wait(barrier, lines + 1)

    def block(at, sem, to):
        return pltpu.make_async_remote_copy(
            src_ref=xg.at[at], dst_ref=xg.at[at], send_sem=gsend.at[sem], recv_sem=grecv.at[at],
            device_id=to, device_id_type=MESH,
        )

    order = sorted(range(1, lines), key=lambda step: min(step, lines - step))
    sends = []
    for step in order:
        sends.append(block(me, step, {"fin": line_at(step) * PAIR + y}))
    sends.append(block(me, 0, y_peer))
    for send in sends:
        send.start()
    for step in order:
        source = line_at(lines - step) * PAIR + y
        passed = block(source, lines - 1 + step, y_peer)
        passed.wait_recv()
        passed.start()
        sends.append(passed)
    for step in range(lines):
        block(line_at(lines - step) * PAIR + (1 - y), 0, y_peer).wait_recv()

    for line in range(lines):
        pair = [xg[line * PAIR + k].astype(jnp.float32) for k in range(PAIR)]
        to = pl.ds(line * PAIR * rows, PAIR * rows)
        xs[to, pl.ds(0, fold)] = jnp.concatenate(
            [b[:rows, :fold] for b in pair], axis=0).astype(jnp.bfloat16)
        xs[to, pl.ds(fold, fold)] = jnp.concatenate(
            [b[rows:, :fold] for b in pair], axis=0).astype(jnp.bfloat16)
        idc[to, :] = jnp.concatenate([b[:rows, fold:] for b in pair], axis=0)

    swaps = []

    def project(g, weight, start, size):
        loads[g].wait()

        def tile(t, carry):
            src = pl.ds(pl.multiple_of(start + t * TILE, TILE), TILE)
            dst = pl.ds(pl.multiple_of(t * TILE, TILE), TILE)
            ps[g, :, dst] = jnp.dot(xs[...], weight[:, src], preferred_element_type=jnp.float32)
            return carry

        lax.fori_loop(0, size // TILE, tile, 0)
        swap = pltpu.make_async_remote_copy(
            src_ref=ps.at[g], dst_ref=pr.at[g], send_sem=psend.at[g], recv_sem=precv.at[g],
            device_id=sibling, device_id_type=MESH,
        )
        swap.start()
        swaps.append(swap)

    def activate(g):
        swaps[parts + g].wait_recv()
        total = ps[parts + g] + pr[parts + g]
        total = 0.5 * total * (1.0 + lax.erf(total * math.sqrt(0.5)))
        hid[:, pl.ds(g * up_w, up_w)] = total.astype(jnp.bfloat16)

    for part in range(parts):
        project(part, wq_v.at[part], 0, cols)
    for g in range(groups):
        project(parts + g, wu_v, g * up_w, up_w)
        if g:
            activate(g - 1)

    for part in range(parts):
        swaps[part].wait_recv()
    diagonal = lax.broadcasted_iota(jnp.int32, (toks, toks), 0) == lax.broadcasted_iota(
        jnp.int32, (toks, toks), 1)
    by_row = idc[:, pl.ds(0, toks)]
    same = by_row == jnp.sum(jnp.where(diagonal, by_row, 0.0), axis=0, keepdims=True)

    def head_norm(v):
        m = jnp.mean(v, -1, keepdims=True)
        s = jnp.mean(v * v, -1, keepdims=True)
        return ((v - m) * lax.rsqrt(s - m * m + 1e-06)).astype(jnp.bfloat16)

    for h in range(cols // HEAD):
        at = pl.ds(h * HEAD, HEAD)
        q, k, v = [(ps[i, :, at] + pr[i, :, at]).astype(jnp.bfloat16) for i in range(3)]
        qn, kn = head_norm(q.astype(jnp.float32)), head_norm(k.astype(jnp.float32))
        scores = lax.dot_general(
            qn, kn, (((1,), (1,)), ((), ())), preferred_element_type=jnp.float32
        ) * (1.0 / math.sqrt(HEAD))
        e = jnp.where(same, jnp.exp(scores), 0.0).astype(jnp.bfloat16)
        den = jnp.sum(e.astype(jnp.float32), -1, keepdims=True)
        total = jnp.dot(e, v, preferred_element_type=jnp.float32)
        att[:, at] = (total / den).astype(jnp.bfloat16)
    activate(groups - 1)

    loads[base].wait()
    reduces = []

    def line_rows(line, who):
        return pl.ds(pl.multiple_of(line * (PAIR * rows) + who * rows, rows), rows)

    def to_pair(j):
        at = pl.ds(j * out_w, out_w)
        theirs = jnp.concatenate([p[line_rows(k, 1 - y), at] for k in range(lines)], axis=0)
        ys[j] = theirs.astype(jnp.bfloat16)
        copy = pltpu.make_async_remote_copy(
            src_ref=ys.at[j], dst_ref=yr.at[j], send_sem=ysend.at[j], recv_sem=yrecv.at[j],
            device_id=y_peer, device_id_type=MESH,
        )
        copy.start()
        return copy

    def to_line(j, arrived):
        arrived.wait_recv()
        at = pl.ds(j * out_w, out_w)
        got = yr[j].astype(jnp.float32)
        for k in range(lines):
            total = p[line_rows(k, y), at] + got[k * rows:(k + 1) * rows]
            own[k, :, at] = total
            zs[j, k] = jnp.concatenate(
                [total[:, :out_w // 2], total[:, out_w // 2:]], axis=0).astype(jnp.bfloat16)
        copies = []
        for step in range(1, lines):
            line = line_at(step)
            copy = pltpu.make_async_remote_copy(
                src_ref=zs.at[j, line], dst_ref=zr.at[j, step - 1],
                send_sem=zsend.at[j, step - 1], recv_sem=zrecv.at[j, step - 1],
                device_id={"fin": line * PAIR + y}, device_id_type=MESH,
            )
            copy.start()
            copies.append(copy)
        reduces.append(copies)

    pairs = []
    for j in range(chunks):
        loads[base + 1 + j].wait()

        def tile(t, carry):
            at = pl.ds(pl.multiple_of(j * out_w + t * TILE, TILE), TILE)
            p[:, at] = jnp.dot(
                att[...], wo_v[:, at], preferred_element_type=jnp.float32
            ) + jnp.dot(hid[...], wd_v[:, at], preferred_element_type=jnp.float32)
            return carry

        lax.fori_loop(0, out_w // TILE, tile, 0)
        pairs.append(to_pair(j))
        if j >= LAG:
            to_line(j - LAG, pairs[j - LAG])
    for j in range(chunks - LAG, chunks):
        to_line(j, pairs[j])

    for j in range(chunks):
        at = pl.ds(j * out_w, out_w)
        total = own[z, :, at]
        for copy_at, copy in enumerate(reduces[j]):
            copy.wait_recv()
            got = zr[j, copy_at].astype(jnp.float32)
            total = total + jnp.concatenate([got[:rows], got[rows:]], axis=1)
        residual = tokens[:, pl.ds(pl.multiple_of(core * half + j * out_w, LANES), out_w)]
        out[:, at] = (residual.astype(jnp.float32) + total).astype(jnp.bfloat16)

    for copy in sends + swaps + pairs:
        copy.wait_send()
    for copies in reduces:
        for copy in copies:
            copy.wait_send()


def fused(lines, tokens, segment_ids, norm_gain, w_qkv, w_up, w_out, w_down):
    rows = tokens.shape[0]
    half, parts, cols = w_qkv.shape
    wide = w_up.shape[1]
    count = lines * PAIR
    toks = rows * count
    groups = wide // cols
    chunks = half // cols
    out_w = half // chunks
    bf16, f32 = jnp.bfloat16, jnp.float32
    dma = pltpu.SemaphoreType.DMA
    vmem = pl.BlockSpec(memory_space=pltpu.VMEM)
    hbm = pl.BlockSpec(memory_space=pl.ANY)
    macs = toks * (half * (parts * cols + wide) + (cols + wide) * half)
    return pl.pallas_call(
        functools.partial(fused_kernel, lines, groups, chunks),
        out_shape=jax.ShapeDtypeStruct((rows, half), bf16),
        in_specs=[vmem, pl.BlockSpec(memory_space=pltpu.SMEM), vmem, hbm, hbm, hbm, hbm],
        out_specs=vmem,
        scratch_shapes=[
            pltpu.VMEM((parts, half, cols), bf16),
            pltpu.VMEM((half, wide), bf16),
            pltpu.VMEM((cols, half), bf16),
            pltpu.VMEM((wide, half), bf16),
            pltpu.VMEM((count, 2 * rows, half // 2 + LANES), bf16),
            pltpu.VMEM((toks, half), bf16),
            pltpu.VMEM((toks, LANES), f32),
            pltpu.VMEM((parts + groups, toks, cols), f32),
            pltpu.VMEM((parts + groups, toks, cols), f32),
            pltpu.VMEM((toks, cols), bf16),
            pltpu.VMEM((toks, wide), bf16),
            pltpu.VMEM((toks, half), f32),
            pltpu.VMEM((chunks, toks // PAIR, out_w), bf16),
            pltpu.VMEM((chunks, toks // PAIR, out_w), bf16),
            pltpu.VMEM((chunks, lines, 2 * rows, out_w // 2), bf16),
            pltpu.VMEM((chunks, lines - 1, 2 * rows, out_w // 2), bf16),
            pltpu.VMEM((lines, rows, half), f32),
            dma((parts + groups + 1 + chunks,)),
            dma((2 * lines - 1,)),
            dma((count,)),
            dma((parts + groups,)),
            dma((parts + groups,)),
            dma((chunks,)),
            dma((chunks,)),
            dma((chunks, lines - 1)),
            dma((chunks, lines - 1)),
        ],
        compiler_params=pltpu.CompilerParams(
            collective_id=0, has_side_effects=True, vmem_limit_bytes=VMEM_LIMIT
        ),
        cost_estimate=pl.CostEstimate(
            flops=2 * macs, bytes_accessed=2 * macs // toks, transcendentals=0
        ),
    )(
        tokens, segment_ids, norm_gain.reshape(1, -1), jnp.transpose(w_qkv, (1, 0, 2)),
        w_up, w_out, w_down,
    )


VMEM_LIMIT = 63 << 20


def feature_norm(values):
    center = jnp.mean(values, -1, keepdims=True)
    square = jnp.mean(values * values, -1, keepdims=True)
    return (values - center) * lax.rsqrt(square - center * center + 1e-06)


def attend(qkv_local, query_ids):
    spread = lax.all_to_all(qkv_local, "fin", split_axis=0, concat_axis=2, tiled=True)
    spread = spread.reshape(spread.shape[0], 3, -1, HEAD)
    query = feature_norm(spread[:, 0].astype(jnp.float32)).astype(jnp.bfloat16)
    keys = feature_norm(spread[:, 1].astype(jnp.float32)).astype(jnp.bfloat16)
    value = spread[:, 2]
    tok_rows, heads, head_size = query.shape
    factor = 1.0 / math.sqrt(head_size)
    marks = query_ids + 1
    key_part = lax.all_gather(keys, "fin", axis=0, tiled=True)
    value_part = lax.all_gather(value, "fin", axis=0, tiled=True)
    mark_part = lax.all_gather(marks, "fin", axis=0, tiled=True)
    scores = (
        jnp.einsum("qhd,khd->hqk", query, key_part, preferred_element_type=jnp.float32) * factor
    )
    same = marks[:, None] == mark_part[None, :]
    weight = jnp.where(same[None], jnp.exp(scores), 0.0).astype(jnp.bfloat16)
    den = jnp.sum(weight.astype(jnp.float32), -1)
    total = jnp.einsum("hqk,khd->qhd", weight, value_part, preferred_element_type=jnp.float32)
    total, den = (total, den)
    attended = (total / jnp.transpose(den)[:, :, None]).astype(jnp.bfloat16)
    return attended.reshape(tok_rows, heads * head_size)


def local(tokens, segment_ids, norm_gain, w_qkv, w_up, w_out, w_down):
    values = tokens.astype(jnp.float32)
    normed_full = (feature_norm(values) * norm_gain).astype(jnp.bfloat16)
    half_width = w_qkv.shape[0]
    offset = lax.axis_index("fout") * half_width
    normed = lax.dynamic_slice_in_dim(normed_full, offset, half_width, 1)
    residual = lax.dynamic_slice_in_dim(values, offset, half_width, 1)
    parts, columns = (w_qkv.shape[1], w_qkv.shape[2])
    qkv_cols = parts * columns
    qkv_matrix = w_qkv.reshape(half_width, qkv_cols)
    piece = lax.all_gather(normed, "fin", axis=0, tiled=True)
    first = jnp.dot(piece, qkv_matrix, preferred_element_type=jnp.float32)
    second = jnp.dot(piece, w_up, preferred_element_type=jnp.float32)
    partial_value = jnp.concatenate([first, second], axis=1)
    qkv_part = partial_value[:, :qkv_cols].reshape(partial_value.shape[0], parts, columns)
    up_part = partial_value[:, qkv_cols:]
    qkv_sum, up_sum = lax.psum((qkv_part, up_part), "fout")
    attended = attend(qkv_sum.astype(jnp.bfloat16), segment_ids)
    hidden = jax.nn.gelu(up_sum, approximate=False).astype(jnp.bfloat16)
    head_block = lax.all_to_all(attended, "fin", split_axis=1, concat_axis=0, tiled=True)
    first = jnp.dot(head_block, w_out, preferred_element_type=jnp.float32)
    mixed = lax.psum_scatter(
        first + jnp.dot(hidden, w_down, preferred_element_type=jnp.float32),
        "fin",
        scatter_dimension=0,
        tiled=True,
    )
    return (residual + mixed).astype(jnp.bfloat16)


def fits(mesh, tokens, w_qkv, w_up, w_out):
    fin, rows = mesh.shape["fin"], tokens.shape[0] // (mesh.shape["grp"] * mesh.shape["fin"])
    half, cols = w_qkv.shape[0] // mesh.shape["fout"], w_qkv.shape[2] // fin
    wide = w_up.shape[1] // fin
    weights = 2 * half * (w_qkv.shape[1] * cols + cols + 2 * wide)
    return (
        mesh.shape["fout"] == 2 and fin % PAIR == 0 and fin > PAIR and rows == 8
        and rows * fin <= LANES and cols % TILE == 0 and cols % HEAD == 0
        and wide % cols == 0 and half % cols == 0 and half // cols >= LAG and weights <= 56 << 20
    )


def solution(mesh):
    def run(*args):
        tokens, _, _, w_qkv, w_up, w_out, _ = args
        if fits(mesh, tokens, w_qkv, w_up, w_out):
            body = functools.partial(fused, mesh.shape["fin"] // PAIR)
        else:
            body = local
        return placed(mesh, body)(*args)

    return run


def placed(mesh, body):
    return jax.shard_map(
        body,
        mesh=mesh,
        in_specs=(
            P(("grp", "fin"), None),
            P(("grp", "fin")),
            P(),
            P("fout", None, "fin"),
            P("fout", "fin"),
            P("fin", "fout"),
            P("fin", "fout"),
        ),
        out_specs=P(("grp", "fin"), "fout"),
        check_vma=False,
    )
```
